32 devices in a mesh: grp: 2 (over x), ctx: 8 (over z, y), head: 2 (over core).
Axes of the slice: x: 2, y: 2, z: 4, core: 2. Of those that a mesh axis runs over, the one named last changes fastest.
Arguments:
- cache_keys: bfloat16 [16, 8, 2048, 128], P('grp', 'head', 'ctx'), parts along dimension 0, may hold values from -4 to 4
- cache_values: bfloat16 [16, 8, 2048, 128], P('grp', 'head', 'ctx'), parts along dimension 0, may hold values from -8 to 8
- ref_queries: bfloat16 [16, 8, 256, 128], P('grp', 'head'), parts along dimension 0, may hold values from -264 to 264
- listed: int32 [16, 8, 128], P('grp', 'head'), parts along dimension 0, may hold values from 0 to 2047, as said below
Outputs:
- compact_keys: bfloat16 [16, 8, 128, 128], P('grp', 'head'), parts along dimension 0
- compact_values: bfloat16 [16, 8, 128, 128], P('grp', 'head'), parts along dimension 0
The draws below stay inside these ranges and needn't reach their ends.
There are 2 independent parts, one for each index of `grp`. The reference program is written for one: setup_inputs(seed, part) draws one part's arguments, and reference() takes and returns one part's arrays. A program takes and returns all parts, laid end to end along the dimension named above; each array names one. Nothing has to cross between parts.
Inputs may be any that keep to these rules, and one draw needn't show every extreme that they name: `listed`: for each layer and head the 128 positions are distinct; at most 16 of them lie in one aligned block of 256 positions, and exactly 16 in some block.
All inputs are finite; a program needn't handle non-finite values.
Results may differ from the reference program's by a relative error of at most 0.0046.
Values may be sent and summed in bfloat16 or wider, within the bound.
A program may use at most 64 MiB of HBM per device.

```python
import math
import jax
import jax.numpy as jnp
from jax import lax

HD = 128
KV_HEADS = 8
LAYERS = 8
TOK_DEV = 256
NQ = 256
KEEP = 128
CAP = 16
SLAB = 2048


def listed_positions(key):
    base = jax.random.fold_in(key, 7)
    shard_count = SLAB // TOK_DEV
    count = LAYERS * KV_HEADS
    key_one, key_two, key_three, key_four = jax.random.split(base, 4)
    order_scores = jax.random.randint(key_one, (count, shard_count, TOK_DEV), 0, 2 ** 20) * TOK_DEV
    order_scores = order_scores + jnp.arange(TOK_DEV, dtype=jnp.int32)[None, None, :]
    offsets = jnp.argsort(order_scores, axis=-1)[:, :, :CAP].astype(jnp.int32)
    shard_bias = jax.random.randint(key_two, (count, shard_count), 0, 4)
    hottest = jax.random.randint(key_three, (count,), 0, shard_count)
    shard_bias = jnp.where(jnp.arange(shard_count)[None, :] == hottest[:, None], 4, shard_bias)
    noise = jax.random.randint(key_four, (count, shard_count, CAP), 0, 2 ** 16)
    flat_index = jnp.arange(shard_count * CAP, dtype=jnp.int32).reshape(1, shard_count, CAP)
    ranked = shard_bias[:, :, None] * 2 ** 22 + noise * (shard_count * CAP) + flat_index
    chosen = lax.top_k(ranked.reshape(count, shard_count * CAP), KEEP)[1].astype(jnp.int32)
    home_shard = chosen // CAP
    within = jnp.take_along_axis(offsets.reshape(count, shard_count * CAP), chosen, axis=1)
    return (home_shard * TOK_DEV + within).reshape(LAYERS, KV_HEADS, KEEP).astype(jnp.int32)


def drawn_pair(key):
    base = jax.random.fold_in(key, 5)
    key_one, key_two = jax.random.split(base, 2)
    shape = (LAYERS, KV_HEADS, SLAB, HD)
    key_table = jax.random.truncated_normal(key_one, -4.0, 4.0, shape, jnp.float32)
    queries = 1.5 * jax.random.truncated_normal(key_two, -4.0, 4.0, (LAYERS, KV_HEADS, NQ, HD), jnp.float32)
    return (key_table, queries)


def draw_cache_keys(key, part):
    return drawn_pair(key)[0].astype(jnp.bfloat16)


def draw_ref_queries(key, part):
    return drawn_pair(key)[1].astype(jnp.bfloat16)


def draw_listed(key, part):
    return listed_positions(key)


def levels(rng, dims, shards, smallest, largest):
    loudness = 1.0
    for dim, parts in shards:
        steps = jax.random.uniform(jax.random.fold_in(jax.random.fold_in(rng, 6), dim), (parts,), jnp.float32, smallest / len(shards), largest / len(shards))
        loudness = loudness * jnp.repeat(jnp.exp(steps), dims[dim] // parts).reshape((-1,) + (1,) * (len(dims) - 1 - dim))
    return loudness


def scatter_about(rng, shape, deviation, most, shards=(), held_as=jnp.bfloat16):
    values = jax.random.normal(rng, shape, jnp.float32) * deviation
    if len(shards) > 0:
        values = levels(rng, shape, shards, -0.22, 0.18) * values
    return jnp.clip(values, min=-most, max=most).astype(held_as)


def setup_inputs(seed: int = 0, part: int = 0) -> dict:
    keys = jax.random.split(jax.random.key(seed), 5)
    own_keys = jax.random.split(jax.random.fold_in(keys[4], part), 5)
    return {
        "cache_keys": draw_cache_keys(jax.random.fold_in(jax.random.fold_in(keys[4], part), 71), part),
        "cache_values": scatter_about(own_keys[1], (LAYERS, KV_HEADS, SLAB, HD), 2.0, 8.0, ((1, 2), (2, 8))),
        "ref_queries": draw_ref_queries(jax.random.fold_in(jax.random.fold_in(keys[4], part), 71), part),
        "listed": draw_listed(jax.random.fold_in(jax.random.fold_in(keys[4], part), 71), part),
    }


ridge_share = 0.05

def fit_one(pieces):
    queries, key_table, value_table, positions = pieces
    score_scale = 1.0 / math.sqrt(HD)
    scores = jnp.dot(queries.astype(jnp.float32), key_table.T.astype(jnp.float32), preferred_element_type=jnp.float32) * score_scale
    row_peak = lax.optimization_barrier(jnp.max(scores, axis=-1, keepdims=True))
    expw = jnp.exp(scores - row_peak)
    totals = lax.optimization_barrier(jnp.sum(expw, axis=-1))
    weighted = jnp.dot(expw.astype(jnp.bfloat16).astype(jnp.float32), value_table.astype(jnp.float32), preferred_element_type=jnp.float32)
    target = weighted / totals[:, None]
    picked = jnp.take(key_table, positions.astype(jnp.int32), axis=0)
    compact_scores = jnp.dot(queries.astype(jnp.float32), picked.T.astype(jnp.float32), preferred_element_type=jnp.float32) * score_scale
    fit_weights = jax.nn.softmax(compact_scores, axis=-1)
    gram_matrix = jnp.dot(fit_weights.T, fit_weights, precision=lax.Precision.HIGHEST)
    moments = jnp.dot(fit_weights.T, target, precision=lax.Precision.HIGHEST)
    ridge_term = ridge_share * jnp.trace(gram_matrix) / KEEP
    system = gram_matrix + ridge_term * jnp.eye(KEEP, dtype=jnp.float32)
    factor = jnp.linalg.cholesky(system)
    halfway = lax.linalg.triangular_solve(factor, moments, left_side=True, lower=True)
    solved = lax.linalg.triangular_solve(factor, halfway, left_side=True, lower=True, transpose_a=True)
    return (picked, solved.astype(jnp.bfloat16))

def reference(cache_keys, cache_values, ref_queries, listed):
    count = LAYERS * KV_HEADS
    query_rows = ref_queries.reshape(count, NQ, HD)
    key_rows = cache_keys.reshape(count, SLAB, HD)
    value_rows = cache_values.reshape(count, SLAB, HD)
    positions = listed.reshape(count, KEEP)
    picked, solved = lax.map(fit_one, (query_rows, key_rows, value_rows, positions))
    return (picked.reshape(LAYERS, KV_HEADS, KEEP, HD), solved.reshape(LAYERS, KV_HEADS, KEEP, HD))
```

```python
import functools
import math

import jax
import jax.numpy as jnp
from jax import lax
from jax.experimental import pallas as pl
from jax.experimental.pallas import tpu as pltpu
from jax.sharding import PartitionSpec as P

ridge_share = 0.05
block_rows = 16
MESH = pl.DeviceIdType.MESH
EXACT = lax.Precision.HIGHEST
f32, bf16 = jnp.float32, jnp.bfloat16


def dot(a, b, dims, precision=None):
    return lax.dot_general(
        a, b, ((dims[:1], dims[1:]), ((), ())), precision=precision, preferred_element_type=f32
    )


def spectrum_steps(keep):
    low = 1.0 / (1.0 + keep / ridge_share)
    lows = []
    while 1.0 - low > 1e-7:
        lows.append(low)
        low = 4.0 * low / (1.0 + low) ** 2
    return lows


def kernel(
    n, keys, values, queries, listed, out_keys, out_values,
    local_pos, slot_code, rows_send, rows_recv, own_sum, own_stats,
    w1_send, w1_recv, s1_send, s1_recv, w2_send, w2_recv, s2_send, s2_recv, fit_map,
    rows_ss, rows_rs, w1_ss, w1_rs, s1_ss, s1_rs, w2_ss, w2_rs, s2_ss, s2_rs,
    kz_ss, kz_rs, ky_ss, ky_rs, vz_ss, vz_rs, vy_ss, vy_rs,
):
    items, tok, head = keys.shape
    query_count = queries.shape[1]
    keep = listed.shape[1]
    nz = n // 2
    ipl = items // n
    scale = 1.0 / math.sqrt(head)
    me = lax.axis_index("ctx")
    z, y = me // 2, lax.rem(me, 2)
    mate = 2 * z + 1 - y

    def copy(src, dst, ss, rs, to):
        return pltpu.make_async_remote_copy(
            src_ref=src, dst_ref=dst, send_sem=ss, recv_sem=rs,
            device_id={"ctx": to}, device_id_type=MESH,
        )

    def z_of(k):
        return lax.rem(z + 1 + k, nz)

    barrier = pltpu.get_barrier_semaphore()
    for d in range(1, n):
        pl.semaphore_signal(
            barrier, inc=1, device_id={"ctx": lax.rem(me + d, n)}, device_id_type=MESH
        )

    def attend(item):
        scores = dot(keys[item], queries[item], (1, 1))
        peak = jnp.max(scores, axis=0, keepdims=True)
        expw = jnp.exp((scores - peak) * scale)
        total = jnp.sum(expw, axis=0, keepdims=True)
        return dot(values[item], expw.astype(bf16), (0, 0)), peak, total

    before = jnp.where(
        lax.broadcasted_iota(jnp.int32, (keep, keep), 0)
        < lax.broadcasted_iota(jnp.int32, (keep, keep), 1), 1.0, 0.0,
    ).astype(bf16)
    pos = listed[...] - me * tok
    is_local = (pos >= 0) & (pos < tok)
    rank = dot(jnp.where(is_local, 1.0, 0.0).astype(bf16), before, (1, 0))
    local_pos[...] = pos
    slot_code[...] = jnp.where(is_local, rank, -1.0)
    slot_iota = lax.broadcasted_iota(jnp.int32, (block_rows, keep), 0).astype(f32)
    tok_iota = lax.broadcasted_iota(jnp.int32, (tok, keep), 0)

    def pick_rows(owner, _):
        for j in range(ipl):
            item = owner * ipl + j
            slots = jnp.where(slot_iota == slot_code[pl.ds(item, 1), :], 1.0, 0.0).astype(bf16)
            at = jnp.where(tok_iota == local_pos[pl.ds(item, 1), :], 1.0, 0.0).astype(bf16)
            chosen = dot(slots, at, (1, 1)).astype(bf16)
            rows_send[owner, j] = dot(chosen, keys[item], (1, 0)).astype(bf16)
        return 0

    def send_one(k):
        owner = 2 * z_of(k) + 1 - y
        for j in range(ipl):
            total_w, peak, total = attend(owner * ipl + j)
            w1_send[k, j] = total_w.astype(bf16)
            s1_send[k, 0, pl.ds(j, 1), :] = peak
            s1_send[k, 1, pl.ds(j, 1), :] = total

    def w1(k):
        return copy(w1_send.at[k], w1_recv.at[k], w1_ss.at[k], w1_rs.at[k], mate)

    def s1(k):
        return copy(s1_send.at[k], s1_recv.at[k], s1_ss.at[k], s1_rs.at[k], mate)

    def w2(k):
        to = 2 * z_of(k) + y
        return copy(w2_send.at[k], w2_recv.at[k], w2_ss.at[k], w2_rs.at[k], to)

    def s2(k):
        to = 2 * z_of(k) + y
        return copy(s2_send.at[k], s2_recv.at[k], s2_ss.at[k], s2_rs.at[k], to)

    def rows_copy(d):
        to = lax.rem(me + d, n)
        return copy(rows_send.at[to], rows_recv.at[me], rows_ss.at[d - 1], rows_rs.at[d - 1], to)

    def block(ref, owner):
        return ref.at[pl.ds(owner * ipl, ipl)]

    def to_z(ref, ss, rs, d):
        mine = block(ref, me)
        return copy(mine, mine, ss.at[d - 1], rs.at[d - 1], 2 * lax.rem(z + d, nz) + y)

    def to_mate(ref, ss, rs, d):
        part = block(ref, 2 * lax.rem(z - d + nz, nz) + y)
        return copy(part, part, ss.at[d], rs.at[d], mate)

    def each(low, high, step):
        def body(k, _):
            step(k)
            return 0

        lax.fori_loop(low, high, body, 0)

    send_one(0)
    pl.semaphore_wait(barrier, n - 1)
    w1(0).start()
    s1(0).start()

    def send_next(k):
        send_one(k)
        w1(k).start()
        s1(k).start()

    each(1, nz, send_next)
    lax.fori_loop(0, n, pick_rows, 0)
    each(1, n, lambda d: rows_copy(d).start())
    rows_recv[me] = rows_send[me]

    def keep_own(k):
        owner = 2 * z_of(k) + y
        for j in range(ipl):
            total_w, peak, total = attend(owner * ipl + j)
            own_sum[k, j] = total_w
            own_stats[k, 0, pl.ds(j, 1), :] = peak
            own_stats[k, 1, pl.ds(j, 1), :] = total

    each(0, nz, keep_own)

    each(1, n, lambda d: rows_copy(d).wait())
    shard_iota = lax.broadcasted_iota(jnp.int32, (n, keep), 0)
    row_iota = lax.broadcasted_iota(jnp.int32, (n * block_rows, keep), 0).astype(f32)
    gathered_rows = [
        rows_recv[:, j].reshape(n * block_rows, head) for j in range(ipl)
    ]
    for j in range(ipl):
        item = me * ipl + j
        where_listed = listed[pl.ds(item, 1), :]
        first = shard_iota * tok
        home = jnp.where((where_listed >= first) & (where_listed < first + tok), 1.0, 0.0)
        earlier = dot(home.astype(bf16), before, (1, 0))
        code = jnp.sum(
            home * (earlier + block_rows * shard_iota.astype(f32)), axis=0, keepdims=True
        )
        place = jnp.where(row_iota == code, 1.0, 0.0).astype(bf16)
        out_keys[item] = dot(place, gathered_rows[j], (0, 0)).astype(bf16)
    each(1, nz, lambda d: to_z(out_keys, kz_ss, kz_rs, d).start())

    diagonal = lax.broadcasted_iota(jnp.int32, (keep, keep), 0) == lax.broadcasted_iota(
        jnp.int32, (keep, keep), 1
    )
    unit = jnp.where(diagonal, 1.0, 0.0).astype(f32)
    fits, systems, inverses = [], [], []
    for j in range(ipl):
        item = me * ipl + j
        scores = dot(out_keys[item], queries[item], (1, 1))
        expw = jnp.exp((scores - jnp.max(scores, axis=0, keepdims=True)) * scale)
        fit = expw / jnp.sum(expw, axis=0, keepdims=True)
        gram = dot(fit, fit, (1, 1), EXACT)
        trace = jnp.sum(jnp.where(diagonal, gram, 0.0), keepdims=True)
        ridge = ridge_share * trace / keep
        bound = trace + ridge
        fits.append(fit)
        systems.append((gram + ridge * unit) / bound)
        inverses.append(unit / bound)
    lows = spectrum_steps(keep)
    for step, low in enumerate(lows):
        gain = 4.0 / (1.0 + low) ** 2
        for j in range(ipl):
            factor = gain * (1.0 + low) * unit - gain * systems[j]
            if step == 0:
                inverses[j] = factor * jnp.sum(
                    jnp.where(diagonal, inverses[j], 0.0), keepdims=True
                ) / keep
            else:
                inverses[j] = dot(factor, inverses[j], (1, 0), EXACT)
            if step < len(lows) - 1:
                systems[j] = dot(factor, systems[j], (1, 0), EXACT)
    for j in range(ipl):
        fit_map[j] = dot(inverses[j], fits[j], (1, 0), EXACT)

    def merged(k, j):
        peak_a, total_a = own_stats[k, 0, pl.ds(j, 1), :], own_stats[k, 1, pl.ds(j, 1), :]
        peak_b, total_b = s1_recv[k, 0, pl.ds(j, 1), :], s1_recv[k, 1, pl.ds(j, 1), :]
        peak = jnp.maximum(peak_a, peak_b)
        share_a = jnp.exp((peak_a - peak) * scale)
        share_b = jnp.exp((peak_b - peak) * scale)
        total_w = own_sum[k, j] * share_a + w1_recv[k, j].astype(f32) * share_b
        return total_w, peak, total_a * share_a + total_b * share_b

    def pass_on(k):
        w1(k).wait()
        s1(k).wait()
        for j in range(ipl):
            total_w, peak, total = merged(k, j)
            w2_send[k, j] = total_w.astype(bf16)
            s2_send[k, 0, pl.ds(j, 1), :] = peak
            s2_send[k, 1, pl.ds(j, 1), :] = total
        w2(k).start()
        s2(k).start()

    each(0, nz - 1, pass_on)
    w1(nz - 1).wait()
    s1(nz - 1).wait()

    to_mate(out_keys, ky_ss, ky_rs, 0).start()

    def keys_on(d):
        to_z(out_keys, kz_ss, kz_rs, d).wait()
        to_mate(out_keys, ky_ss, ky_rs, d).start()

    each(1, nz, keys_on)

    for j in range(ipl):
        total_w, peak, total = merged(nz - 1, j)
        own_sum[nz - 1, j] = total_w
        own_stats[nz - 1, 0, pl.ds(j, 1), :] = peak
        own_stats[nz - 1, 1, pl.ds(j, 1), :] = total

    def take_in(k):
        w2(k).wait()
        s2(k).wait()
        for j in range(ipl):
            peak_a = own_stats[nz - 1, 0, pl.ds(j, 1), :]
            peak_b = s2_recv[k, 0, pl.ds(j, 1), :]
            peak = jnp.maximum(peak_a, peak_b)
            share_a = jnp.exp((peak_a - peak) * scale)
            share_b = jnp.exp((peak_b - peak) * scale)
            own_sum[nz - 1, j] = own_sum[nz - 1, j] * share_a + w2_recv[k, j].astype(f32) * share_b
            own_stats[nz - 1, 0, pl.ds(j, 1), :] = peak
            own_stats[nz - 1, 1, pl.ds(j, 1), :] = (
                own_stats[nz - 1, 1, pl.ds(j, 1), :] * share_a
                + s2_recv[k, 1, pl.ds(j, 1), :] * share_b
            )

    each(0, nz - 1, take_in)
    for j in range(ipl):
        target = own_sum[nz - 1, j] / own_stats[nz - 1, 1, pl.ds(j, 1), :]
        out_values[me * ipl + j] = dot(fit_map[j], target, (1, 1), EXACT).astype(bf16)

    each(1, nz, lambda d: to_z(out_values, vz_ss, vz_rs, d).start())
    to_mate(out_values, vy_ss, vy_rs, 0).start()

    def values_on(d):
        to_z(out_values, vz_ss, vz_rs, d).wait()
        to_mate(out_values, vy_ss, vy_rs, d).start()

    each(1, nz, values_on)

    def finish(d):
        to_mate(out_keys, ky_ss, ky_rs, d).wait()
        to_mate(out_values, vy_ss, vy_rs, d).wait()

    each(0, nz, finish)


def shards(cache_keys, cache_values, ref_queries, listed):
    layer_count, head_count, tok, head = cache_keys.shape
    query_count, keep = ref_queries.shape[2], listed.shape[2]
    items = layer_count * head_count
    n = lax.axis_size("ctx")
    nz, ipl = n // 2, items // n
    vmem = pl.BlockSpec(memory_space=pltpu.VMEM)
    dma = pltpu.SemaphoreType.DMA
    out = jax.ShapeDtypeStruct((items, keep, head), bf16)
    sums = (ipl, head, query_count)
    stats = (2, ipl, query_count)
    scratch = [
        pltpu.VMEM((items, keep), jnp.int32),
        pltpu.VMEM((items, keep), f32),
        pltpu.VMEM((n, ipl, block_rows, head), bf16),
        pltpu.VMEM((n, ipl, block_rows, head), bf16),
        pltpu.VMEM((nz,) + sums, f32),
        pltpu.VMEM((nz,) + stats, f32),
        pltpu.VMEM((nz,) + sums, bf16),
        pltpu.VMEM((nz,) + sums, bf16),
        pltpu.VMEM((nz,) + stats, f32),
        pltpu.VMEM((nz,) + stats, f32),
        pltpu.VMEM((nz - 1,) + sums, bf16),
        pltpu.VMEM((nz - 1,) + sums, bf16),
        pltpu.VMEM((nz - 1,) + stats, f32),
        pltpu.VMEM((nz - 1,) + stats, f32),
        pltpu.VMEM((ipl, keep, query_count), f32),
    ]
    for count in (n - 1, nz, nz, nz - 1, nz - 1, nz - 1, nz, nz - 1, nz):
        scratch += [dma((count,)), dma((count,))]
    compact, solved = pl.pallas_call(
        functools.partial(kernel, n),
        out_shape=(out, out),
        in_specs=[vmem] * 4,
        out_specs=(vmem, vmem),
        scratch_shapes=scratch,
        compiler_params=pltpu.CompilerParams(
            collective_id=0, has_side_effects=True, vmem_limit_bytes=48 * 2**20
        ),
        name="compact_fit",
    )(
        cache_keys.reshape(items, tok, head),
        cache_values.reshape(items, tok, head),
        ref_queries.reshape(items, query_count, head),
        listed.reshape(items, keep),
    )
    shape = (layer_count, head_count, keep, head)
    return compact.reshape(shape), solved.reshape(shape)


def solution(mesh):
    in_specs = (
        P("grp", "head", "ctx", None),
        P("grp", "head", "ctx", None),
        P("grp", "head", None, None),
        P("grp", "head", None),
    )
    out_specs = (P("grp", "head", None, None), P("grp", "head", None, None))
    return jax.shard_map(shards, mesh=mesh, in_specs=in_specs, out_specs=out_specs, check_vma=False)
```

```python
import functools
import math

import jax
import jax.numpy as jnp
from jax import lax
from jax.experimental import pallas as pl
from jax.experimental.pallas import tpu as pltpu
from jax.sharding import PartitionSpec as P

ridge_share = 0.05
block_rows = 16
MESH = pl.DeviceIdType.MESH
EXACT = lax.Precision.HIGHEST
f32, bf16 = jnp.float32, jnp.bfloat16


def dot(a, b, dims, precision=None):
    return lax.dot_general(
        a, b, ((dims[:1], dims[1:]), ((), ())), precision=precision, preferred_element_type=f32
    )


def spectrum_steps(keep):
    low = 1.0 / (1.0 + keep / ridge_share)
    lows = []
    while 1.0 - low > 1e-7:
        lows.append(low)
        low = 4.0 * low / (1.0 + low) ** 2
    return lows


def kernel(
    n, keys, values, queries, listed, out_keys, out_values,
    local_pos, slot_code, rows_send, rows_recv, own_sum, own_stats,
    sum_send, sum_recv, stat_send, stat_recv, fit_map,
    rows_ss, rows_rs, sum_ss, sum_rs, stat_ss, stat_rs, key_ss, key_rs, val_ss, val_rs,
):
    items, tok, head = keys.shape
    keep = listed.shape[1]
    ipl = items // n
    bits = n.bit_length() - 1
    scale = 1.0 / math.sqrt(head)
    me = lax.axis_index("ctx")

    def copy(src, dst, ss, rs, to):
        return pltpu.make_async_remote_copy(
            src_ref=src, dst_ref=dst, send_sem=ss, recv_sem=rs,
            device_id={"ctx": to}, device_id_type=MESH,
        )

    def other(r):
        return sum(
            lax.rem(me // 2**b + r // 2**b, 2) * 2**b for b in range(bits)
        )

    def low_bit(r):
        return (r & -r).bit_length() - 1

    barrier = pltpu.get_barrier_semaphore()
    for d in range(1, n):
        pl.semaphore_signal(
            barrier, inc=1, device_id={"ctx": lax.rem(me + d, n)}, device_id_type=MESH
        )

    def attend(item):
        scores = dot(keys[item], queries[item], (1, 1))
        peak = jnp.max(scores, axis=0, keepdims=True)
        expw = jnp.exp((scores - peak) * scale)
        total = jnp.sum(expw, axis=0, keepdims=True)
        return dot(values[item], expw.astype(bf16), (0, 0)), peak, total

    before = jnp.where(
        lax.broadcasted_iota(jnp.int32, (keep, keep), 0)
        < lax.broadcasted_iota(jnp.int32, (keep, keep), 1), 1.0, 0.0,
    ).astype(bf16)
    pos = listed[...] - me * tok
    is_local = (pos >= 0) & (pos < tok)
    rank = dot(jnp.where(is_local, 1.0, 0.0).astype(bf16), before, (1, 0))
    local_pos[...] = pos
    slot_code[...] = jnp.where(is_local, rank, -1.0)
    slot_iota = lax.broadcasted_iota(jnp.int32, (block_rows, keep), 0).astype(f32)
    tok_iota = lax.broadcasted_iota(jnp.int32, (tok, keep), 0)

    def pick_rows(owner, _):
        for j in range(ipl):
            item = owner * ipl + j
            slots = jnp.where(slot_iota == slot_code[pl.ds(item, 1), :], 1.0, 0.0).astype(bf16)
            at = jnp.where(tok_iota == local_pos[pl.ds(item, 1), :], 1.0, 0.0).astype(bf16)
            chosen = dot(slots, at, (1, 1)).astype(bf16)
            rows_send[owner, j] = dot(chosen, keys[item], (1, 0)).astype(bf16)
        return 0

    def rows_copy(d):
        to = lax.rem(me + d, n)
        return copy(rows_send.at[to], rows_recv.at[me], rows_ss.at[d - 1], rows_rs.at[d - 1], to)

    def sum_copies(r, step):
        to = other(step)
        return (
            copy(sum_send.at[r], sum_recv.at[r], sum_ss.at[r], sum_rs.at[r], to),
            copy(stat_send.at[r], stat_recv.at[r], stat_ss.at[r], stat_rs.at[r], to),
        )

    def block_copy(ref, ss, rs, r):
        step = r & -r
        part = ref.at[pl.ds(other(r ^ step) * ipl, ipl)]
        return copy(part, part, ss.at[r], rs.at[r], other(step))

    def key_copy(r):
        return block_copy(out_keys, key_ss, key_rs, r)

    def value_copy(r):
        return block_copy(out_values, val_ss, val_rs, r)

    def each(low, high, step):
        def body(k, _):
            step(k)
            return 0

        lax.fori_loop(low, high, body, 0)

    def put_stats(ref, r, j, peak, total):
        ref[r, 0, pl.ds(j, 1), :] = peak
        ref[r, 1, pl.ds(j, 1), :] = total

    def get_stats(ref, r, j):
        return ref[r, 0, pl.ds(j, 1), :], ref[r, 1, pl.ds(j, 1), :]

    def send_group(k):
        r = n - 1 - 2 * k
        owner = other(r)
        for j in range(ipl):
            weighted, peak, total = attend(owner * ipl + j)
            sum_send[r, j] = weighted.astype(bf16)
            put_stats(stat_send, r, j, peak, total)

    def start_group(k):
        for sent in sum_copies(n - 1 - 2 * k, 1):
            sent.start()

    def send_next(k):
        send_group(k)
        start_group(k)

    def keep_group(k):
        owner = other(2 * k)
        for j in range(ipl):
            weighted, peak, total = attend(owner * ipl + j)
            own_sum[k, j] = weighted
            put_stats(own_stats, k, j, peak, total)

    def merge(r):
        sources = [r + 2**b for b in range(bits if r == 0 else low_bit(r))]
        for source in sources:
            for sent in sum_copies(source, source - r):
                sent.wait()
            if source == 1:
                for odd in range(1, n, 2):
                    key_copy(odd).start()
            for j in range(ipl):
                peak_a, total_a = get_stats(own_stats, r // 2, j)
                peak_b, total_b = get_stats(stat_recv, source, j)
                peak = jnp.maximum(peak_a, peak_b)
                share_a = jnp.exp((peak_a - peak) * scale)
                share_b = jnp.exp((peak_b - peak) * scale)
                weighted = own_sum[r // 2, j] * share_a + sum_recv[source, j].astype(f32) * share_b
                total = total_a * share_a + total_b * share_b
                if r > 0 and source == sources[-1]:
                    sum_send[r, j] = weighted.astype(bf16)
                    put_stats(stat_send, r, j, peak, total)
                else:
                    own_sum[r // 2, j] = weighted
                    put_stats(own_stats, r // 2, j, peak, total)
        if r > 0:
            for sent in sum_copies(r, r & -r):
                sent.start()

    send_group(0)
    pl.semaphore_wait(barrier, n - 1)
    start_group(0)
    each(1, n // 2, send_next)
    lax.fori_loop(0, n, pick_rows, 0)
    each(1, n, lambda d: rows_copy(d).start())
    rows_recv[me] = rows_send[me]
    each(0, n // 2, keep_group)

    evens = list(range(n - 2, 0, -2))
    early = evens[: (len(evens) + 1) // 2]
    merge(early[0])

    each(1, n, lambda d: rows_copy(d).wait())
    shard_iota = lax.broadcasted_iota(jnp.int32, (n, keep), 0)
    row_iota = lax.broadcasted_iota(jnp.int32, (n * block_rows, keep), 0).astype(f32)
    for j in range(ipl):
        item = me * ipl + j
        where_listed = listed[pl.ds(item, 1), :]
        first = shard_iota * tok
        home = jnp.where((where_listed >= first) & (where_listed < first + tok), 1.0, 0.0)
        earlier = dot(home.astype(bf16), before, (1, 0))
        code = jnp.sum(
            home * (earlier + block_rows * shard_iota.astype(f32)), axis=0, keepdims=True
        )
        place = jnp.where(row_iota == code, 1.0, 0.0).astype(bf16)
        rows = rows_recv[:, j].reshape(n * block_rows, head)
        out_keys[item] = dot(place, rows, (0, 0)).astype(bf16)
    for b in range(bits - 1, 0, -1):
        key_copy(2**b).start()
    for r in early[1:]:
        merge(r)

    diagonal = lax.broadcasted_iota(jnp.int32, (keep, keep), 0) == lax.broadcasted_iota(
        jnp.int32, (keep, keep), 1
    )
    unit = jnp.where(diagonal, 1.0, 0.0).astype(f32)
    fits, systems, inverses = [], [], []
    for j in range(ipl):
        item = me * ipl + j
        scores = dot(out_keys[item], queries[item], (1, 1))
        expw = jnp.exp((scores - jnp.max(scores, axis=0, keepdims=True)) * scale)
        fit = expw / jnp.sum(expw, axis=0, keepdims=True)
        gram = dot(fit, fit, (1, 1), EXACT)
        trace = jnp.sum(jnp.where(diagonal, gram, 0.0), keepdims=True)
        ridge = ridge_share * trace / keep
        bound = trace + ridge
        fits.append(fit)
        systems.append((gram + ridge * unit) / bound)
        inverses.append(1.0 / bound)
    lows = spectrum_steps(keep)
    for step, low in enumerate(lows):
        gain = 4.0 / (1.0 + low) ** 2
        for j in range(ipl):
            factor = gain * (1.0 + low) * unit - gain * systems[j]
            if step == 0:
                inverses[j] = factor * inverses[j]
            else:
                inverses[j] = dot(factor, inverses[j], (1, 0), EXACT)
            if step < len(lows) - 1:
                systems[j] = dot(factor, systems[j], (1, 0), EXACT)
    for j in range(ipl):
        fit_map[j] = dot(inverses[j], fits[j], (1, 0), EXACT)

    for r in evens[len(early):]:
        merge(r)

    arrivals = sorted(range(2, n, 2), key=lambda r: (bin(r).count("1"), -r))
    for r in arrivals:
        key_copy(r).wait()
        for b in range(low_bit(r) - 1, 0, -1):
            key_copy(r + 2**b).start()
    merge(0)
    for j in range(ipl):
        target = own_sum[0, j] / own_stats[0, 1, pl.ds(j, 1), :]
        out_values[me * ipl + j] = dot(fit_map[j], target, (1, 1), EXACT).astype(bf16)

    for b in range(bits - 1, -1, -1):
        value_copy(2**b).start()
    for r in arrivals:
        value_copy(r).wait()
        for b in range(low_bit(r) - 1, -1, -1):
            value_copy(r + 2**b).start()
    for r in range(1, n, 2):
        key_copy(r).wait()
        value_copy(r).wait()


def shards(cache_keys, cache_values, ref_queries, listed):
    layer_count, head_count, tok, head = cache_keys.shape
    query_count, keep = ref_queries.shape[2], listed.shape[2]
    items = layer_count * head_count
    n = lax.axis_size("ctx")
    ipl = items // n
    vmem = pl.BlockSpec(memory_space=pltpu.VMEM)
    dma = pltpu.SemaphoreType.DMA
    out = jax.ShapeDtypeStruct((items, keep, head), bf16)
    sums = (ipl, head, query_count)
    stats = (2, ipl, query_count)
    scratch = [
        pltpu.VMEM((items, keep), jnp.int32),
        pltpu.VMEM((items, keep), f32),
        pltpu.VMEM((n, ipl, block_rows, head), bf16),
        pltpu.VMEM((n, ipl, block_rows, head), bf16),
        pltpu.VMEM((n // 2,) + sums, f32),
        pltpu.VMEM((n // 2,) + stats, f32),
        pltpu.VMEM((n,) + sums, bf16),
        pltpu.VMEM((n,) + sums, bf16),
        pltpu.VMEM((n,) + stats, f32),
        pltpu.VMEM((n,) + stats, f32),
        pltpu.VMEM((ipl, keep, query_count), f32),
    ]
    scratch += [dma((n,))] * 10
    compact, solved = pl.pallas_call(
        functools.partial(kernel, n),
        out_shape=(out, out),
        in_specs=[vmem] * 4,
        out_specs=(vmem, vmem),
        scratch_shapes=scratch,
        compiler_params=pltpu.CompilerParams(
            collective_id=0, has_side_effects=True, vmem_limit_bytes=48 * 2**20
        ),
        name="compact_fit",
    )(
        cache_keys.reshape(items, tok, head),
        cache_values.reshape(items, tok, head),
        ref_queries.reshape(items, query_count, head),
        listed.reshape(items, keep),
    )
    shape = (layer_count, head_count, keep, head)
    return compact.reshape(shape), solved.reshape(shape)


def solution(mesh):
    in_specs = (
        P("grp", "head", "ctx", None),
        P("grp", "head", "ctx", None),
        P("grp", "head", None, None),
        P("grp", "head", None),
    )
    out_specs = (P("grp", "head", None, None), P("grp", "head", None, None))
    return jax.shard_map(shards, mesh=mesh, in_specs=in_specs, out_specs=out_specs, check_vma=False)
```

```python
import functools
import math

import jax
import jax.numpy as jnp
from jax import lax
from jax.experimental import pallas as pl
from jax.experimental.pallas import tpu as pltpu
from jax.sharding import PartitionSpec as P

ridge_share = 0.05
block_rows = 16
MESH = pl.DeviceIdType.MESH
EXACT = lax.Precision.HIGHEST
f32, bf16 = jnp.float32, jnp.bfloat16


def dot(a, b, dims, precision=None):
    return lax.dot_general(
        a, b, ((dims[:1], dims[1:]), ((), ())), precision=precision, preferred_element_type=f32
    )


def spectrum_steps(keep):
    low = 1.0 / (1.0 + keep / ridge_share)
    lows = []
    while 1.0 - low > 1e-7:
        lows.append(low)
        low = 4.0 * low / (1.0 + low) ** 2
    return lows


def kernel(
    n, keys, values, queries, listed, out_keys, out_values,
    local_pos, slot_code, rows_send, rows_recv, own_sum, own_stats,
    sum_send, sum_recv, stat_send, stat_recv, fit_map,
    rows_ss, rows_rs, sum_ss, sum_rs, stat_ss, stat_rs, key_ss, key_rs, val_ss, val_rs,
):
    items, tok, head = keys.shape
    keep = listed.shape[1]
    ipl = items // n
    bits = n.bit_length() - 1
    scale = 1.0 / math.sqrt(head)
    me = lax.axis_index("ctx")

    def copy(src, dst, ss, rs, to):
        return pltpu.make_async_remote_copy(
            src_ref=src, dst_ref=dst, send_sem=ss, recv_sem=rs,
            device_id={"ctx": to}, device_id_type=MESH,
        )

    def other(r):
        return sum(
            lax.rem(me // 2**b + r // 2**b, 2) * 2**b for b in range(bits)
        )

    def low_bit(r):
        return (r & -r).bit_length() - 1

    barrier = pltpu.get_barrier_semaphore()
    for d in range(1, n):
        pl.semaphore_signal(
            barrier, inc=1, device_id={"ctx": lax.rem(me + d, n)}, device_id_type=MESH
        )

    def attend(item):
        scores = dot(keys[item], queries[item], (1, 1))
        peak = jnp.max(scores, axis=0, keepdims=True)
        expw = jnp.exp((scores - peak) * scale)
        total = jnp.sum(expw, axis=0, keepdims=True)
        return dot(values[item], expw.astype(bf16), (0, 0)), peak, total

    before = jnp.where(
        lax.broadcasted_iota(jnp.int32, (keep, keep), 0)
        < lax.broadcasted_iota(jnp.int32, (keep, keep), 1), 1.0, 0.0,
    ).astype(bf16)
    pos = listed[...] - me * tok
    is_local = (pos >= 0) & (pos < tok)
    rank = dot(jnp.where(is_local, 1.0, 0.0).astype(bf16), before, (1, 0))
    local_pos[...] = pos
    slot_code[...] = jnp.where(is_local, rank, -1.0)
    slot_iota = lax.broadcasted_iota(jnp.int32, (block_rows, keep), 0).astype(f32)
    tok_iota = lax.broadcasted_iota(jnp.int32, (tok, keep), 0)

    def pick_rows(owner, _):
        for j in range(ipl):
            item = owner * ipl + j
            slots = jnp.where(slot_iota == slot_code[pl.ds(item, 1), :], 1.0, 0.0).astype(bf16)
            at = jnp.where(tok_iota == local_pos[pl.ds(item, 1), :], 1.0, 0.0).astype(bf16)
            chosen = dot(slots, at, (1, 1)).astype(bf16)
            rows_send[owner, j] = dot(chosen, keys[item], (1, 0)).astype(bf16)
        return 0

    def rows_copy(d):
        to = lax.rem(me + d, n)
        return copy(rows_send.at[to], rows_recv.at[me], rows_ss.at[d - 1], rows_rs.at[d - 1], to)

    def sum_copies(r, step):
        to = other(step)
        return (
            copy(sum_send.at[r], sum_recv.at[r], sum_ss.at[r], sum_rs.at[r], to),
            copy(stat_send.at[r], stat_recv.at[r], stat_ss.at[r], stat_rs.at[r], to),
        )

    def block_copy(ref, ss, rs, r):
        step = r & -r
        part = ref.at[pl.ds(other(r ^ step) * ipl, ipl)]
        return copy(part, part, ss.at[r], rs.at[r], other(step))

    def key_copy(r):
        return block_copy(out_keys, key_ss, key_rs, r)

    def value_copy(r):
        return block_copy(out_values, val_ss, val_rs, r)

    def each(low, high, step):
        def body(k, _):
            step(k)
            return 0

        lax.fori_loop(low, high, body, 0)

    def put_stats(ref, r, j, peak, total):
        ref[r, 0, pl.ds(j, 1), :] = peak
        ref[r, 1, pl.ds(j, 1), :] = total

    def get_stats(ref, r, j):
        return ref[r, 0, pl.ds(j, 1), :], ref[r, 1, pl.ds(j, 1), :]

    def send_group(k):
        r = n - 1 - 2 * k
        owner = other(r)
        for j in range(ipl):
            weighted, peak, total = attend(owner * ipl + j)
            sum_send[r, j] = weighted.astype(bf16)
            put_stats(stat_send, r, j, peak, total)

    def start_group(k):
        for sent in sum_copies(n - 1 - 2 * k, 1):
            sent.start()

    def send_next(k):
        send_group(k)
        start_group(k)

    def keep_group(k):
        owner = other(2 * k)
        for j in range(ipl):
            weighted, peak, total = attend(owner * ipl + j)
            own_sum[k, j] = weighted
            put_stats(own_stats, k, j, peak, total)

    def merge(r):
        sources = [r + 2**b for b in range(bits if r == 0 else low_bit(r))]
        for source in sources:
            for sent in sum_copies(source, source - r):
                sent.wait()
            if source == 1:
                for odd in range(1, n, 2):
                    key_copy(odd).start()
            for j in range(ipl):
                peak_a, total_a = get_stats(own_stats, r // 2, j)
                peak_b, total_b = get_stats(stat_recv, source, j)
                peak = jnp.maximum(peak_a, peak_b)
                share_a = jnp.exp((peak_a - peak) * scale)
                share_b = jnp.exp((peak_b - peak) * scale)
                weighted = own_sum[r // 2, j] * share_a + sum_recv[source, j].astype(f32) * share_b
                total = total_a * share_a + total_b * share_b
                if r > 0 and source == sources[-1]:
                    sum_send[r, j] = weighted.astype(bf16)
                    put_stats(stat_send, r, j, peak, total)
                else:
                    own_sum[r // 2, j] = weighted
                    put_stats(own_stats, r // 2, j, peak, total)
        if r > 0:
            for sent in sum_copies(r, r & -r):
                sent.start()

    send_group(0)
    pl.semaphore_wait(barrier, n - 1)
    start_group(0)
    each(1, n // 2, send_next)
    each(0, n // 2, keep_group)
    evens = list(range(n - 2, 0, -2))
    merge(evens[0])
    lax.fori_loop(0, n, pick_rows, 0)
    each(1, n, lambda d: rows_copy(d).start())
    rows_recv[me] = rows_send[me]
    for r in evens[1:]:
        merge(r)

    each(1, n, lambda d: rows_copy(d).wait())
    shard_iota = lax.broadcasted_iota(jnp.int32, (n, keep), 0)
    row_iota = lax.broadcasted_iota(jnp.int32, (n * block_rows, keep), 0).astype(f32)
    for j in range(ipl):
        item = me * ipl + j
        where_listed = listed[pl.ds(item, 1), :]
        first = shard_iota * tok
        home = jnp.where((where_listed >= first) & (where_listed < first + tok), 1.0, 0.0)
        earlier = dot(home.astype(bf16), before, (1, 0))
        code = jnp.sum(
            home * (earlier + block_rows * shard_iota.astype(f32)), axis=0, keepdims=True
        )
        place = jnp.where(row_iota == code, 1.0, 0.0).astype(bf16)
        rows = rows_recv[:, j].reshape(n * block_rows, head)
        out_keys[item] = dot(place, rows, (0, 0)).astype(bf16)
    for b in range(bits - 1, 0, -1):
        key_copy(2**b).start()

    diagonal = lax.broadcasted_iota(jnp.int32, (keep, keep), 0) == lax.broadcasted_iota(
        jnp.int32, (keep, keep), 1
    )
    unit = jnp.where(diagonal, 1.0, 0.0).astype(f32)
    fits, pairs = [], []
    for j in range(ipl):
        item = me * ipl + j
        scores = dot(out_keys[item], queries[item], (1, 1))
        expw = jnp.exp((scores - jnp.max(scores, axis=0, keepdims=True)) * scale)
        fit = expw / jnp.sum(expw, axis=0, keepdims=True)
        gram = dot(fit, fit, (1, 1), EXACT)
        trace = jnp.sum(jnp.where(diagonal, gram, 0.0), keepdims=True)
        ridge = ridge_share * trace / keep
        bound = trace + ridge
        fits.append(fit)
        system = (gram + ridge * unit) / bound
        pairs.append((system, unit / bound))
    lows = spectrum_steps(keep)
    for step, low in enumerate(lows):
        gain = 4.0 / (1.0 + low) ** 2
        for j in range(ipl):
            system, inverse = pairs[j]
            factor = gain * (1.0 + low) * unit - gain * system
            if step == len(lows) - 1:
                fit_map[j] = dot(factor, dot(inverse, fits[j], (1, 0), EXACT), (1, 0), EXACT)
            else:
                both = dot(
                    factor, jnp.concatenate([system, inverse], axis=1), (1, 0), EXACT
                )
                pairs[j] = (both[:, :keep], both[:, keep:])

    arrivals = sorted(range(2, n, 2), key=lambda r: (bin(r).count("1"), -r))
    for r in arrivals:
        key_copy(r).wait()
        for b in range(low_bit(r) - 1, 0, -1):
            key_copy(r + 2**b).start()
    merge(0)
    for j in range(ipl):
        target = own_sum[0, j] / own_stats[0, 1, pl.ds(j, 1), :]
        out_values[me * ipl + j] = dot(fit_map[j], target, (1, 1), EXACT).astype(bf16)

    for b in range(bits - 1, -1, -1):
        value_copy(2**b).start()
    for r in arrivals:
        value_copy(r).wait()
        for b in range(low_bit(r) - 1, -1, -1):
            value_copy(r + 2**b).start()
    for r in range(1, n, 2):
        key_copy(r).wait()
        value_copy(r).wait()


def shards(cache_keys, cache_values, ref_queries, listed):
    layer_count, head_count, tok, head = cache_keys.shape
    query_count, keep = ref_queries.shape[2], listed.shape[2]
    items = layer_count * head_count
    n = lax.axis_size("ctx")
    ipl = items // n
    vmem = pl.BlockSpec(memory_space=pltpu.VMEM)
    dma = pltpu.SemaphoreType.DMA
    out = jax.ShapeDtypeStruct((items, keep, head), bf16)
    sums = (ipl, head, query_count)
    stats = (2, ipl, query_count)
    scratch = [
        pltpu.VMEM((items, keep), jnp.int32),
        pltpu.VMEM((items, keep), f32),
        pltpu.VMEM((n, ipl, block_rows, head), bf16),
        pltpu.VMEM((n, ipl, block_rows, head), bf16),
        pltpu.VMEM((n // 2,) + sums, f32),
        pltpu.VMEM((n // 2,) + stats, f32),
        pltpu.VMEM((n,) + sums, bf16),
        pltpu.VMEM((n,) + sums, bf16),
        pltpu.VMEM((n,) + stats, f32),
        pltpu.VMEM((n,) + stats, f32),
        pltpu.VMEM((ipl, keep, query_count), f32),
    ]
    scratch += [dma((n,))] * 10
    compact, solved = pl.pallas_call(
        functools.partial(kernel, n),
        out_shape=(out, out),
        in_specs=[vmem] * 4,
        out_specs=(vmem, vmem),
        scratch_shapes=scratch,
        compiler_params=pltpu.CompilerParams(
            collective_id=0, has_side_effects=True, vmem_limit_bytes=48 * 2**20
        ),
        name="compact_fit",
    )(
        cache_keys.reshape(items, tok, head),
        cache_values.reshape(items, tok, head),
        ref_queries.reshape(items, query_count, head),
        listed.reshape(items, keep),
    )
    shape = (layer_count, head_count, keep, head)
    return compact.reshape(shape), solved.reshape(shape)


def solution(mesh):
    in_specs = (
        P("grp", "head", "ctx", None),
        P("grp", "head", "ctx", None),
        P("grp", "head", None, None),
        P("grp", "head", None),
    )
    out_specs = (P("grp", "head", None, None), P("grp", "head", None, None))
    return jax.shard_map(shards, mesh=mesh, in_specs=in_specs, out_specs=out_specs, check_vma=False)
```

```python
import functools
import math

import jax
import jax.numpy as jnp
from jax import lax
from jax.experimental import pallas as pl
from jax.experimental.pallas import tpu as pltpu
from jax.sharding import PartitionSpec as P

ridge_share = 0.05
block_rows = 16
MESH = pl.DeviceIdType.MESH
EXACT = lax.Precision.HIGHEST
f32, bf16 = jnp.float32, jnp.bfloat16


def dot(a, b, dims, precision=None):
    return lax.dot_general(
        a, b, ((dims[:1], dims[1:]), ((), ())), precision=precision, preferred_element_type=f32
    )


def split(x):
    first = x.astype(bf16)
    rest = x - first.astype(f32)
    second = rest.astype(bf16)
    return first, second, (rest - second.astype(f32)).astype(bf16)


def product(a, b):
    a1, a2, a3 = split(a)
    b1, b2, b3 = split(b)
    a12 = jnp.concatenate([a1, a2], axis=1)
    a13 = jnp.concatenate([a1, a3], axis=1)
    low = dot(a13, jnp.concatenate([b3, b1], axis=0), (1, 0))
    low += dot(a12, jnp.concatenate([b2, b2], axis=0), (1, 0))
    return low + dot(a12, jnp.concatenate([b1, b1], axis=0), (1, 0))


def spectrum_steps(keep):
    low = 1.0 / (1.0 + keep / ridge_share)
    lows = []
    while 1.0 - low > 1e-7:
        lows.append(low)
        low = 4.0 * low / (1.0 + low) ** 2
    return lows


def kernel(
    n, keys, values, queries, listed, out_keys, out_values,
    local_pos, slot_code, rows_send, rows_recv, own_sum, own_stats,
    sum_send, sum_recv, stat_send, stat_recv, fit_map,
    rows_ss, rows_rs, sum_ss, sum_rs, stat_ss, stat_rs, key_ss, key_rs, val_ss, val_rs,
):
    items, tok, head = keys.shape
    keep = listed.shape[1]
    ipl = items // n
    bits = n.bit_length() - 1
    scale = math.log2(math.e) / math.sqrt(head)
    me = lax.axis_index("ctx")

    def copy(src, dst, ss, rs, to):
        return pltpu.make_async_remote_copy(
            src_ref=src, dst_ref=dst, send_sem=ss, recv_sem=rs,
            device_id={"ctx": to}, device_id_type=MESH,
        )

    def other(r):
        return sum(
            lax.rem(me // 2**b + r // 2**b, 2) * 2**b for b in range(bits)
        )

    def low_bit(r):
        return (r & -r).bit_length() - 1

    barrier = pltpu.get_barrier_semaphore()
    for d in range(1, n):
        pl.semaphore_signal(
            barrier, inc=1, device_id={"ctx": lax.rem(me + d, n)}, device_id_type=MESH
        )

    def attend(item):
        scores = dot(keys[item], queries[item], (1, 1))
        peak = jnp.max(scores, axis=0, keepdims=True)
        expw = jnp.exp2((scores - peak) * scale)
        total = jnp.sum(expw, axis=0, keepdims=True)
        return dot(values[item], expw.astype(bf16), (0, 0)), peak, total

    before = jnp.where(
        lax.broadcasted_iota(jnp.int32, (keep, keep), 0)
        < lax.broadcasted_iota(jnp.int32, (keep, keep), 1), 1.0, 0.0,
    ).astype(bf16)
    pos = listed[...] - me * tok
    is_local = (pos >= 0) & (pos < tok)
    rank = dot(jnp.where(is_local, 1.0, 0.0).astype(bf16), before, (1, 0))
    local_pos[...] = pos
    slot_code[...] = jnp.where(is_local, rank, -1.0)
    slot_iota = lax.broadcasted_iota(jnp.int32, (block_rows, keep), 0).astype(f32)
    tok_iota = lax.broadcasted_iota(jnp.int32, (tok, keep), 0)

    def pick_rows(owner, _):
        for j in range(ipl):
            item = owner * ipl + j
            slots = jnp.where(slot_iota == slot_code[pl.ds(item, 1), :], 1.0, 0.0).astype(bf16)
            at = jnp.where(tok_iota == local_pos[pl.ds(item, 1), :], 1.0, 0.0).astype(bf16)
            chosen = dot(slots, at, (1, 1)).astype(bf16)
            rows_send[owner, j] = dot(chosen, keys[item], (1, 0)).astype(bf16)
        return 0

    def rows_copy(d):
        to = lax.rem(me + d, n)
        return copy(rows_send.at[to], rows_recv.at[me], rows_ss.at[d - 1], rows_rs.at[d - 1], to)

    def sum_copies(r, step):
        to = other(step)
        return (
            copy(sum_send.at[r], sum_recv.at[r], sum_ss.at[r], sum_rs.at[r], to),
            copy(stat_send.at[r], stat_recv.at[r], stat_ss.at[r], stat_rs.at[r], to),
        )

    def block_copy(ref, ss, rs, r):
        step = r & -r
        part = ref.at[pl.ds(other(r ^ step) * ipl, ipl)]
        return copy(part, part, ss.at[r], rs.at[r], other(step))

    def key_copy(r):
        return block_copy(out_keys, key_ss, key_rs, r)

    def value_copy(r):
        return block_copy(out_values, val_ss, val_rs, r)

    def each(low, high, step):
        def body(k, _):
            step(k)
            return 0

        lax.fori_loop(low, high, body, 0)

    def put_stats(ref, r, j, peak, total):
        ref[r, 0, pl.ds(j, 1), :] = peak
        ref[r, 1, pl.ds(j, 1), :] = total

    def get_stats(ref, r, j):
        return ref[r, 0, pl.ds(j, 1), :], ref[r, 1, pl.ds(j, 1), :]

    def send_group(k):
        r = n - 1 - 2 * k
        owner = other(r)
        for j in range(ipl):
            weighted, peak, total = attend(owner * ipl + j)
            sum_send[r, j] = weighted.astype(bf16)
            put_stats(stat_send, r, j, peak, total)

    def start_group(k):
        for sent in sum_copies(n - 1 - 2 * k, 1):
            sent.start()

    def send_next(k):
        send_group(k)
        start_group(k)

    def keep_group(k):
        owner = other(2 * k)
        for j in range(ipl):
            weighted, peak, total = attend(owner * ipl + j)
            own_sum[k, j] = weighted
            put_stats(own_stats, k, j, peak, total)

    def merge(r):
        sources = [r + 2**b for b in range(bits if r == 0 else low_bit(r))]
        for source in sources:
            for sent in sum_copies(source, source - r):
                sent.wait()
            if source == 1:
                for odd in range(1, n, 2):
                    key_copy(odd).start()
            for j in range(ipl):
                peak_a, total_a = get_stats(own_stats, r // 2, j)
                peak_b, total_b = get_stats(stat_recv, source, j)
                peak = jnp.maximum(peak_a, peak_b)
                share_a = jnp.exp2((peak_a - peak) * scale)
                share_b = jnp.exp2((peak_b - peak) * scale)
                weighted = own_sum[r // 2, j] * share_a + sum_recv[source, j].astype(f32) * share_b
                total = total_a * share_a + total_b * share_b
                if r > 0 and source == sources[-1]:
                    sum_send[r, j] = weighted.astype(bf16)
                    put_stats(stat_send, r, j, peak, total)
                else:
                    own_sum[r // 2, j] = weighted
                    put_stats(own_stats, r // 2, j, peak, total)
        if r > 0:
            for sent in sum_copies(r, r & -r):
                sent.start()

    send_group(0)
    pl.semaphore_wait(barrier, n - 1)
    start_group(0)
    each(1, n // 2, send_next)
    each(0, n // 2, keep_group)
    evens = list(range(n - 2, 0, -2))
    merge(evens[0])
    lax.fori_loop(0, n, pick_rows, 0)
    each(1, n, lambda d: rows_copy(d).start())
    rows_recv[me] = rows_send[me]
    for r in evens[1:]:
        merge(r)

    each(1, n, lambda d: rows_copy(d).wait())
    shard_iota = lax.broadcasted_iota(jnp.int32, (n, keep), 0)
    row_iota = lax.broadcasted_iota(jnp.int32, (n * block_rows, keep), 0).astype(f32)
    for j in range(ipl):
        item = me * ipl + j
        where_listed = listed[pl.ds(item, 1), :]
        first = shard_iota * tok
        home = jnp.where((where_listed >= first) & (where_listed < first + tok), 1.0, 0.0)
        earlier = dot(home.astype(bf16), before, (1, 0))
        code = jnp.sum(
            home * (earlier + block_rows * shard_iota.astype(f32)), axis=0, keepdims=True
        )
        place = jnp.where(row_iota == code, 1.0, 0.0).astype(bf16)
        rows = rows_recv[:, j].reshape(n * block_rows, head)
        out_keys[item] = dot(place, rows, (0, 0)).astype(bf16)
    for b in range(bits - 1, 0, -1):
        key_copy(2**b).start()

    diagonal = lax.broadcasted_iota(jnp.int32, (keep, keep), 0) == lax.broadcasted_iota(
        jnp.int32, (keep, keep), 1
    )
    unit = jnp.where(diagonal, 1.0, 0.0).astype(f32)
    fits, pairs = [], []
    for j in range(ipl):
        item = me * ipl + j
        scores = dot(out_keys[item], queries[item], (1, 1))
        expw = jnp.exp2((scores - jnp.max(scores, axis=0, keepdims=True)) * scale)
        fit = expw / jnp.sum(expw, axis=0, keepdims=True)
        gram = dot(fit, fit, (1, 1), EXACT)
        trace = jnp.sum(jnp.where(diagonal, gram, 0.0), keepdims=True)
        ridge = ridge_share * trace / keep
        bound = trace + ridge
        fits.append(fit)
        system = (gram + ridge * unit) / bound
        pairs.append((system, unit / bound))
    lows = spectrum_steps(keep)
    for step, low in enumerate(lows):
        gain = 4.0 / (1.0 + low) ** 2
        for j in range(ipl):
            system, inverse = pairs[j]
            factor = gain * (1.0 + low) * unit - gain * system
            if step == len(lows) - 1:
                fit_map[j] = product(factor, product(inverse, fits[j]))
            else:
                both = product(factor, jnp.concatenate([system, inverse], axis=1))
                pairs[j] = (both[:, :keep], both[:, keep:])

    arrivals = sorted(range(2, n, 2), key=lambda r: (bin(r).count("1"), -r))
    for r in arrivals:
        key_copy(r).wait()
        for b in range(low_bit(r) - 1, 0, -1):
            key_copy(r + 2**b).start()
    merge(0)
    for j in range(ipl):
        target = own_sum[0, j] / own_stats[0, 1, pl.ds(j, 1), :]
        out_values[me * ipl + j] = dot(fit_map[j], target, (1, 1), EXACT).astype(bf16)

    for b in range(bits - 1, -1, -1):
        value_copy(2**b).start()
    for r in arrivals:
        value_copy(r).wait()
        for b in range(low_bit(r) - 1, -1, -1):
            value_copy(r + 2**b).start()
    for r in range(1, n, 2):
        key_copy(r).wait()
        value_copy(r).wait()


def shards(cache_keys, cache_values, ref_queries, listed):
    layer_count, head_count, tok, head = cache_keys.shape
    query_count, keep = ref_queries.shape[2], listed.shape[2]
    items = layer_count * head_count
    n = lax.axis_size("ctx")
    ipl = items // n
    vmem = pl.BlockSpec(memory_space=pltpu.VMEM)
    dma = pltpu.SemaphoreType.DMA
    out = jax.ShapeDtypeStruct((items, keep, head), bf16)
    sums = (ipl, head, query_count)
    stats = (2, ipl, query_count)
    scratch = [
        pltpu.VMEM((items, keep), jnp.int32),
        pltpu.VMEM((items, keep), f32),
        pltpu.VMEM((n, ipl, block_rows, head), bf16),
        pltpu.VMEM((n, ipl, block_rows, head), bf16),
        pltpu.VMEM((n // 2,) + sums, f32),
        pltpu.VMEM((n // 2,) + stats, f32),
        pltpu.VMEM((n,) + sums, bf16),
        pltpu.VMEM((n,) + sums, bf16),
        pltpu.VMEM((n,) + stats, f32),
        pltpu.VMEM((n,) + stats, f32),
        pltpu.VMEM((ipl, keep, query_count), f32),
    ]
    scratch += [dma((n,))] * 10
    compact, solved = pl.pallas_call(
        functools.partial(kernel, n),
        out_shape=(out, out),
        in_specs=[vmem] * 4,
        out_specs=(vmem, vmem),
        scratch_shapes=scratch,
        compiler_params=pltpu.CompilerParams(
            collective_id=0, has_side_effects=True, vmem_limit_bytes=48 * 2**20
        ),
        name="compact_fit",
    )(
        cache_keys.reshape(items, tok, head),
        cache_values.reshape(items, tok, head),
        ref_queries.reshape(items, query_count, head),
        listed.reshape(items, keep),
    )
    shape = (layer_count, head_count, keep, head)
    return compact.reshape(shape), solved.reshape(shape)


def solution(mesh):
    in_specs = (
        P("grp", "head", "ctx", None),
        P("grp", "head", "ctx", None),
        P("grp", "head", None, None),
        P("grp", "head", None),
    )
    out_specs = (P("grp", "head", None, None), P("grp", "head", None, None))
    return jax.shard_map(shards, mesh=mesh, in_specs=in_specs, out_specs=out_specs, check_vma=False)
```

```python
import functools
import math

import jax
import jax.numpy as jnp
from jax import lax
from jax.experimental import pallas as pl
from jax.experimental.pallas import tpu as pltpu
from jax.sharding import PartitionSpec as P

ridge_share = 0.05
block_rows = 16
MESH = pl.DeviceIdType.MESH
EXACT = lax.Precision.HIGHEST
f32, bf16 = jnp.float32, jnp.bfloat16


def dot(a, b, dims, precision=None):
    return lax.dot_general(
        a, b, ((dims[:1], dims[1:]), ((), ())), precision=precision, preferred_element_type=f32
    )


def split(x):
    first = x.astype(bf16)
    rest = x - first.astype(f32)
    second = rest.astype(bf16)
    return first, second, (rest - second.astype(f32)).astype(bf16)


def product(a, b):
    a1, a2, a3 = split(a)
    b1, b2, b3 = split(b)
    a12 = jnp.concatenate([a1, a2], axis=1)
    a13 = jnp.concatenate([a1, a3], axis=1)
    low = dot(a13, jnp.concatenate([b3, b1], axis=0), (1, 0))
    low += dot(a12, jnp.concatenate([b2, b2], axis=0), (1, 0))
    return low + dot(a12, jnp.concatenate([b1, b1], axis=0), (1, 0))


def spectrum_steps(keep):
    low = 1.0 / (1.0 + keep / ridge_share)
    lows = []
    while 1.0 - low > 1e-7:
        lows.append(low)
        low = 4.0 * low / (1.0 + low) ** 2
    return lows


def kernel(
    n, keys, values, queries, listed, out_keys, out_values,
    local_pos, slot_code, rows_send, rows_recv, own_sum, own_stats,
    sum_send, sum_recv, stat_send, stat_recv, fit_map,
    rows_ss, rows_rs, sum_ss, sum_rs, stat_ss, stat_rs, key_ss, key_rs, val_ss, val_rs,
):
    items, tok, head = keys.shape
    keep = listed.shape[1]
    ipl = items // n
    bits = n.bit_length() - 1
    scale = math.log2(math.e) / math.sqrt(head)
    me = lax.axis_index("ctx")

    def copy(src, dst, ss, rs, to):
        return pltpu.make_async_remote_copy(
            src_ref=src, dst_ref=dst, send_sem=ss, recv_sem=rs,
            device_id={"ctx": to}, device_id_type=MESH,
        )

    def other(r):
        return sum(
            lax.rem(me // 2**b + r // 2**b, 2) * 2**b for b in range(bits)
        )

    def low_bit(r):
        return (r & -r).bit_length() - 1

    barrier = pltpu.get_barrier_semaphore()
    for d in range(1, n):
        pl.semaphore_signal(
            barrier, inc=1, device_id={"ctx": lax.rem(me + d, n)}, device_id_type=MESH
        )

    def attend(item):
        scores = dot(keys[item], queries[item], (1, 1))
        peak = jnp.max(scores, axis=0, keepdims=True)
        expw = jnp.exp2((scores - peak) * scale)
        total = jnp.sum(expw, axis=0, keepdims=True)
        return dot(values[item], expw.astype(bf16), (0, 0)), peak, total

    before = jnp.where(
        lax.broadcasted_iota(jnp.int32, (keep, keep), 0)
        < lax.broadcasted_iota(jnp.int32, (keep, keep), 1), 1.0, 0.0,
    ).astype(bf16)
    pos = listed[...] - me * tok
    is_local = (pos >= 0) & (pos < tok)
    rank = dot(jnp.where(is_local, 1.0, 0.0).astype(bf16), before, (1, 0))
    local_pos[...] = pos
    slot_code[...] = jnp.where(is_local, rank, -1.0)
    slot_iota = lax.broadcasted_iota(jnp.int32, (block_rows, keep), 0).astype(f32)
    tok_iota = lax.broadcasted_iota(jnp.int32, (tok, keep), 0)

    def pick_rows(owner, _):
        for j in range(ipl):
            item = owner * ipl + j
            slots = jnp.where(slot_iota == slot_code[pl.ds(item, 1), :], 1.0, 0.0).astype(bf16)
            at = jnp.where(tok_iota == local_pos[pl.ds(item, 1), :], 1.0, 0.0).astype(bf16)
            chosen = dot(slots, at, (1, 1)).astype(bf16)
            rows_send[owner, j] = dot(chosen, keys[item], (1, 0)).astype(bf16)
        return 0

    def rows_copy(d):
        to = lax.rem(me + d, n)
        return copy(rows_send.at[to], rows_recv.at[me], rows_ss.at[d - 1], rows_rs.at[d - 1], to)

    def sum_copies(r, step):
        to = other(step)
        return (
            copy(sum_send.at[r], sum_recv.at[r], sum_ss.at[r], sum_rs.at[r], to),
            copy(stat_send.at[r], stat_recv.at[r], stat_ss.at[r], stat_rs.at[r], to),
        )

    value_order = list(range(bits - 1, -1, -1))
    key_order = value_order[:-2] + value_order[-2:][::-1]

    def last_bit(r, order):
        return [b for b in order if r >> b & 1][-1]

    def block_copy(ref, ss, rs, r, order):
        step = 2 ** last_bit(r, order)
        part = ref.at[pl.ds(other(r ^ step) * ipl, ipl)]
        return copy(part, part, ss.at[r], rs.at[r], other(step))

    def key_copy(r):
        return block_copy(out_keys, key_ss, key_rs, r, key_order)

    def value_copy(r):
        return block_copy(out_values, val_ss, val_rs, r, value_order)

    def own_on(move, order):
        for b in order:
            move(2**b).start()

    def arrivals(order):
        blocks = sorted(
            range(1, n),
            key=lambda r: (bin(r).count("1"), [order.index(b) for b in order if r >> b & 1]),
        )
        return [
            (r, [r + 2**b for b in order[order.index(last_bit(r, order)) + 1 :]]) for r in blocks
        ]

    def pass_on(move, order):
        for r, later in arrivals(order):
            if later:
                move(r).wait()
                for block in later:
                    move(block).start()

    def finish(move, order):
        for r, later in arrivals(order):
            if not later:
                move(r).wait()

    def each(low, high, step):
        def body(k, _):
            step(k)
            return 0

        lax.fori_loop(low, high, body, 0)

    def put_stats(ref, r, j, peak, total):
        ref[r, 0, pl.ds(j, 1), :] = peak
        ref[r, 1, pl.ds(j, 1), :] = total

    def get_stats(ref, r, j):
        return ref[r, 0, pl.ds(j, 1), :], ref[r, 1, pl.ds(j, 1), :]

    def send_group(k):
        r = n - 1 - 2 * k
        owner = other(r)
        for j in range(ipl):
            weighted, peak, total = attend(owner * ipl + j)
            sum_send[r, j] = weighted.astype(bf16)
            put_stats(stat_send, r, j, peak, total)

    def start_group(k):
        for sent in sum_copies(n - 1 - 2 * k, 1):
            sent.start()

    def send_next(k):
        send_group(k)
        start_group(k)

    def keep_group(k):
        owner = other(2 * k)
        for j in range(ipl):
            weighted, peak, total = attend(owner * ipl + j)
            own_sum[k, j] = weighted
            put_stats(own_stats, k, j, peak, total)

    def merge(r):
        sources = [r + 2**b for b in range(bits if r == 0 else low_bit(r))]
        for source in sources:
            for sent in sum_copies(source, source - r):
                sent.wait()
            for j in range(ipl):
                peak_a, total_a = get_stats(own_stats, r // 2, j)
                peak_b, total_b = get_stats(stat_recv, source, j)
                peak = jnp.maximum(peak_a, peak_b)
                share_a = jnp.exp2((peak_a - peak) * scale)
                share_b = jnp.exp2((peak_b - peak) * scale)
                weighted = own_sum[r // 2, j] * share_a + sum_recv[source, j].astype(f32) * share_b
                total = total_a * share_a + total_b * share_b
                if r > 0 and source == sources[-1]:
                    sum_send[r, j] = weighted.astype(bf16)
                    put_stats(stat_send, r, j, peak, total)
                else:
                    own_sum[r // 2, j] = weighted
                    put_stats(own_stats, r // 2, j, peak, total)
        if r > 0:
            for sent in sum_copies(r, r & -r):
                sent.start()

    send_group(0)
    pl.semaphore_wait(barrier, n - 1)
    start_group(0)
    each(1, n // 2, send_next)
    each(0, n // 2, keep_group)
    evens = list(range(n - 2, 0, -2))
    merge(evens[0])
    lax.fori_loop(0, n, pick_rows, 0)
    each(1, n, lambda d: rows_copy(d).start())
    rows_recv[me] = rows_send[me]
    for r in evens[1:]:
        merge(r)

    each(1, n, lambda d: rows_copy(d).wait())
    shard_iota = lax.broadcasted_iota(jnp.int32, (n, keep), 0)
    row_iota = lax.broadcasted_iota(jnp.int32, (n * block_rows, keep), 0).astype(f32)
    for j in range(ipl):
        item = me * ipl + j
        where_listed = listed[pl.ds(item, 1), :]
        first = shard_iota * tok
        home = jnp.where((where_listed >= first) & (where_listed < first + tok), 1.0, 0.0)
        earlier = dot(home.astype(bf16), before, (1, 0))
        code = jnp.sum(
            home * (earlier + block_rows * shard_iota.astype(f32)), axis=0, keepdims=True
        )
        place = jnp.where(row_iota == code, 1.0, 0.0).astype(bf16)
        rows = rows_recv[:, j].reshape(n * block_rows, head)
        out_keys[item] = dot(place, rows, (0, 0)).astype(bf16)
    own_on(key_copy, key_order)

    diagonal = lax.broadcasted_iota(jnp.int32, (keep, keep), 0) == lax.broadcasted_iota(
        jnp.int32, (keep, keep), 1
    )
    unit = jnp.where(diagonal, 1.0, 0.0).astype(f32)
    fits, pairs = [], []
    for j in range(ipl):
        item = me * ipl + j
        scores = dot(out_keys[item], queries[item], (1, 1))
        expw = jnp.exp2((scores - jnp.max(scores, axis=0, keepdims=True)) * scale)
        fit = expw / jnp.sum(expw, axis=0, keepdims=True)
        gram = dot(fit, fit, (1, 1), EXACT)
        trace = jnp.sum(jnp.where(diagonal, gram, 0.0), keepdims=True)
        ridge = ridge_share * trace / keep
        bound = trace + ridge
        fits.append(fit)
        system = (gram + ridge * unit) / bound
        pairs.append((system, unit / bound))
    lows = spectrum_steps(keep)
    for step, low in enumerate(lows):
        gain = 4.0 / (1.0 + low) ** 2
        for j in range(ipl):
            system, inverse = pairs[j]
            factor = gain * (1.0 + low) * unit - gain * system
            if step == len(lows) - 1:
                fit_map[j] = product(factor, product(inverse, fits[j]))
            else:
                both = product(factor, jnp.concatenate([system, inverse], axis=1))
                pairs[j] = (both[:, :keep], both[:, keep:])

    pass_on(key_copy, key_order)
    merge(0)
    for j in range(ipl):
        target = own_sum[0, j] / own_stats[0, 1, pl.ds(j, 1), :]
        out_values[me * ipl + j] = dot(fit_map[j], target, (1, 1), EXACT).astype(bf16)

    own_on(value_copy, value_order)
    pass_on(value_copy, value_order)
    finish(key_copy, key_order)
    finish(value_copy, value_order)


def shards(cache_keys, cache_values, ref_queries, listed):
    layer_count, head_count, tok, head = cache_keys.shape
    query_count, keep = ref_queries.shape[2], listed.shape[2]
    items = layer_count * head_count
    n = lax.axis_size("ctx")
    ipl = items // n
    vmem = pl.BlockSpec(memory_space=pltpu.VMEM)
    dma = pltpu.SemaphoreType.DMA
    out = jax.ShapeDtypeStruct((items, keep, head), bf16)
    sums = (ipl, head, query_count)
    stats = (2, ipl, query_count)
    scratch = [
        pltpu.VMEM((items, keep), jnp.int32),
        pltpu.VMEM((items, keep), f32),
        pltpu.VMEM((n, ipl, block_rows, head), bf16),
        pltpu.VMEM((n, ipl, block_rows, head), bf16),
        pltpu.VMEM((n // 2,) + sums, f32),
        pltpu.VMEM((n // 2,) + stats, f32),
        pltpu.VMEM((n,) + sums, bf16),
        pltpu.VMEM((n,) + sums, bf16),
        pltpu.VMEM((n,) + stats, f32),
        pltpu.VMEM((n,) + stats, f32),
        pltpu.VMEM((ipl, keep, query_count), f32),
    ]
    scratch += [dma((n,))] * 10
    compact, solved = pl.pallas_call(
        functools.partial(kernel, n),
        out_shape=(out, out),
        in_specs=[vmem] * 4,
        out_specs=(vmem, vmem),
        scratch_shapes=scratch,
        compiler_params=pltpu.CompilerParams(
            collective_id=0, has_side_effects=True, vmem_limit_bytes=48 * 2**20
        ),
        name="compact_fit",
    )(
        cache_keys.reshape(items, tok, head),
        cache_values.reshape(items, tok, head),
        ref_queries.reshape(items, query_count, head),
        listed.reshape(items, keep),
    )
    shape = (layer_count, head_count, keep, head)
    return compact.reshape(shape), solved.reshape(shape)


def solution(mesh):
    in_specs = (
        P("grp", "head", "ctx", None),
        P("grp", "head", "ctx", None),
        P("grp", "head", None, None),
        P("grp", "head", None),
    )
    out_specs = (P("grp", "head", None, None), P("grp", "head", None, None))
    return jax.shard_map(shards, mesh=mesh, in_specs=in_specs, out_specs=out_specs, check_vma=False)
```

```python
import functools
import math

import jax
import jax.numpy as jnp
from jax import lax
from jax.experimental import pallas as pl
from jax.experimental.pallas import tpu as pltpu
from jax.sharding import PartitionSpec as P

ridge_share = 0.05
block_rows = 16
MESH = pl.DeviceIdType.MESH
EXACT = lax.Precision.HIGHEST
f32, bf16 = jnp.float32, jnp.bfloat16


def dot(a, b, dims, precision=None):
    return lax.dot_general(
        a, b, ((dims[:1], dims[1:]), ((), ())), precision=precision, preferred_element_type=f32
    )


def split(x):
    first = x.astype(bf16)
    rest = x - first.astype(f32)
    second = rest.astype(bf16)
    return first, second, (rest - second.astype(f32)).astype(bf16)


def product(a, b):
    a1, a2, a3 = split(a)
    b1, b2, b3 = split(b)
    a12 = jnp.concatenate([a1, a2], axis=1)
    a13 = jnp.concatenate([a1, a3], axis=1)
    low = dot(a13, jnp.concatenate([b3, b1], axis=0), (1, 0))
    low += dot(a12, jnp.concatenate([b2, b2], axis=0), (1, 0))
    return low + dot(a12, jnp.concatenate([b1, b1], axis=0), (1, 0))


def spectrum_steps(keep):
    low = 1.0 / (1.0 + keep / ridge_share)
    lows = []
    while 1.0 - low > 1e-7:
        lows.append(low)
        low = 4.0 * low / (1.0 + low) ** 2
    return lows


def kernel(
    n, all_keys, all_values, all_queries, listed, out_keys, out_values,
    keys, values, queries,    local_pos, slot_code, rows_send, rows_recv, own_sum, own_stats,
    sum_send, sum_recv, stat_send, stat_recv, fit_map,
    rows_ss, rows_rs, sum_ss, sum_rs, stat_ss, stat_rs, key_ss, key_rs, val_ss, val_rs,
    load_sems,
):
    items, tok, head = keys.shape
    keep = listed.shape[1]
    ipl = items // n
    bits = n.bit_length() - 1
    scale = math.log2(math.e) / math.sqrt(head)
    me = lax.axis_index("ctx")

    def copy(src, dst, ss, rs, to):
        return pltpu.make_async_remote_copy(
            src_ref=src, dst_ref=dst, send_sem=ss, recv_sem=rs,
            device_id={"ctx": to}, device_id_type=MESH,
        )

    def other(r):
        return sum(
            lax.rem(me // 2**b + r // 2**b, 2) * 2**b for b in range(bits)
        )

    def low_bit(r):
        return (r & -r).bit_length() - 1

    barrier = pltpu.get_barrier_semaphore()
    for d in range(1, n):
        pl.semaphore_signal(
            barrier, inc=1, device_id={"ctx": lax.rem(me + d, n)}, device_id_type=MESH
        )

    def loads(r):
        part = pl.ds(other(r) * ipl, ipl)
        pairs = ((all_keys, keys), (all_queries, queries), (all_values, values))
        return [
            pltpu.make_async_copy(source.at[part], held.at[part], load_sems.at[i, r])
            for i, (source, held) in enumerate(pairs)
        ]

    def start_loads(r):
        for load in loads(r):
            load.start()

    def wait_loads(r):
        for load in loads(r):
            load.wait()

    for r in list(range(n - 1, 0, -2)) + list(range(0, n, 2)):
        start_loads(r)

    def attend(item):
        scores = dot(keys[item], queries[item], (1, 1))
        peak = jnp.max(scores, axis=0, keepdims=True)
        expw = jnp.exp2((scores - peak) * scale)
        total = jnp.sum(expw, axis=0, keepdims=True)
        return dot(values[item], expw.astype(bf16), (0, 0)), peak, total

    before = jnp.where(
        lax.broadcasted_iota(jnp.int32, (keep, keep), 0)
        < lax.broadcasted_iota(jnp.int32, (keep, keep), 1), 1.0, 0.0,
    ).astype(bf16)
    pos = listed[...] - me * tok
    is_local = (pos >= 0) & (pos < tok)
    rank = dot(jnp.where(is_local, 1.0, 0.0).astype(bf16), before, (1, 0))
    local_pos[...] = pos
    slot_code[...] = jnp.where(is_local, rank, -1.0)
    slot_iota = lax.broadcasted_iota(jnp.int32, (block_rows, keep), 0).astype(f32)
    tok_iota = lax.broadcasted_iota(jnp.int32, (tok, keep), 0)

    def pick_rows(owner, _):
        for j in range(ipl):
            item = owner * ipl + j
            slots = jnp.where(slot_iota == slot_code[pl.ds(item, 1), :], 1.0, 0.0).astype(bf16)
            at = jnp.where(tok_iota == local_pos[pl.ds(item, 1), :], 1.0, 0.0).astype(bf16)
            chosen = dot(slots, at, (1, 1)).astype(bf16)
            rows_send[owner, j] = dot(chosen, keys[item], (1, 0)).astype(bf16)
        return 0

    def rows_copy(d):
        to = lax.rem(me + d, n)
        return copy(rows_send.at[to], rows_recv.at[me], rows_ss.at[d - 1], rows_rs.at[d - 1], to)

    def sum_copies(r, step):
        to = other(step)
        return (
            copy(sum_send.at[r], sum_recv.at[r], sum_ss.at[r], sum_rs.at[r], to),
            copy(stat_send.at[r], stat_recv.at[r], stat_ss.at[r], stat_rs.at[r], to),
        )

    value_order = list(range(bits - 1, -1, -1))
    key_order = value_order[:-2] + value_order[-2:][::-1]

    def last_bit(r, order):
        return [b for b in order if r >> b & 1][-1]

    def block_copy(ref, ss, rs, r, order):
        step = 2 ** last_bit(r, order)
        part = ref.at[pl.ds(other(r ^ step) * ipl, ipl)]
        return copy(part, part, ss.at[r], rs.at[r], other(step))

    def key_copy(r):
        return block_copy(out_keys, key_ss, key_rs, r, key_order)

    def value_copy(r):
        return block_copy(out_values, val_ss, val_rs, r, value_order)

    def own_on(move, order):
        for b in order:
            move(2**b).start()

    def arrivals(order):
        blocks = sorted(
            range(1, n),
            key=lambda r: (bin(r).count("1"), [order.index(b) for b in order if r >> b & 1]),
        )
        return [
            (r, [r + 2**b for b in order[order.index(last_bit(r, order)) + 1 :]]) for r in blocks
        ]

    def pass_on(move, order):
        for r, later in arrivals(order):
            if later:
                move(r).wait()
                for block in later:
                    move(block).start()

    def finish(move, order):
        for r, later in arrivals(order):
            if not later:
                move(r).wait()

    def each(low, high, step):
        def body(k, _):
            step(k)
            return 0

        lax.fori_loop(low, high, body, 0)

    def put_stats(ref, r, j, peak, total):
        ref[r, 0, pl.ds(j, 1), :] = peak
        ref[r, 1, pl.ds(j, 1), :] = total

    def get_stats(ref, r, j):
        return ref[r, 0, pl.ds(j, 1), :], ref[r, 1, pl.ds(j, 1), :]

    def send_group(k):
        r = n - 1 - 2 * k
        owner = other(r)
        wait_loads(r)
        for j in range(ipl):
            weighted, peak, total = attend(owner * ipl + j)
            sum_send[r, j] = weighted.astype(bf16)
            put_stats(stat_send, r, j, peak, total)

    def start_group(k):
        for sent in sum_copies(n - 1 - 2 * k, 1):
            sent.start()

    def send_next(k):
        send_group(k)
        start_group(k)

    def keep_group(k):
        owner = other(2 * k)
        wait_loads(2 * k)
        for j in range(ipl):
            weighted, peak, total = attend(owner * ipl + j)
            own_sum[k, j] = weighted
            put_stats(own_stats, k, j, peak, total)

    def merge(r):
        sources = [r + 2**b for b in range(bits if r == 0 else low_bit(r))]
        for source in sources:
            for sent in sum_copies(source, source - r):
                sent.wait()
            for j in range(ipl):
                peak_a, total_a = get_stats(own_stats, r // 2, j)
                peak_b, total_b = get_stats(stat_recv, source, j)
                peak = jnp.maximum(peak_a, peak_b)
                share_a = jnp.exp2((peak_a - peak) * scale)
                share_b = jnp.exp2((peak_b - peak) * scale)
                weighted = own_sum[r // 2, j] * share_a + sum_recv[source, j].astype(f32) * share_b
                total = total_a * share_a + total_b * share_b
                if r > 0 and source == sources[-1]:
                    sum_send[r, j] = weighted.astype(bf16)
                    put_stats(stat_send, r, j, peak, total)
                else:
                    own_sum[r // 2, j] = weighted
                    put_stats(own_stats, r // 2, j, peak, total)
        if r > 0:
            for sent in sum_copies(r, r & -r):
                sent.start()

    send_group(0)
    pl.semaphore_wait(barrier, n - 1)
    start_group(0)
    each(1, n // 2, send_next)
    each(0, n // 2, keep_group)
    evens = list(range(n - 2, 0, -2))
    merge(evens[0])
    lax.fori_loop(0, n, pick_rows, 0)
    each(1, n, lambda d: rows_copy(d).start())
    rows_recv[me] = rows_send[me]
    for r in evens[1:]:
        merge(r)

    each(1, n, lambda d: rows_copy(d).wait())
    shard_iota = lax.broadcasted_iota(jnp.int32, (n, keep), 0)
    row_iota = lax.broadcasted_iota(jnp.int32, (n * block_rows, keep), 0).astype(f32)
    for j in range(ipl):
        item = me * ipl + j
        where_listed = listed[pl.ds(item, 1), :]
        first = shard_iota * tok
        home = jnp.where((where_listed >= first) & (where_listed < first + tok), 1.0, 0.0)
        earlier = dot(home.astype(bf16), before, (1, 0))
        code = jnp.sum(
            home * (earlier + block_rows * shard_iota.astype(f32)), axis=0, keepdims=True
        )
        place = jnp.where(row_iota == code, 1.0, 0.0).astype(bf16)
        rows = rows_recv[:, j].reshape(n * block_rows, head)
        out_keys[item] = dot(place, rows, (0, 0)).astype(bf16)
    own_on(key_copy, key_order)

    diagonal = lax.broadcasted_iota(jnp.int32, (keep, keep), 0) == lax.broadcasted_iota(
        jnp.int32, (keep, keep), 1
    )
    unit = jnp.where(diagonal, 1.0, 0.0).astype(f32)
    fits, pairs = [], []
    for j in range(ipl):
        item = me * ipl + j
        scores = dot(out_keys[item], queries[item], (1, 1))
        expw = jnp.exp2((scores - jnp.max(scores, axis=0, keepdims=True)) * scale)
        fit = expw / jnp.sum(expw, axis=0, keepdims=True)
        gram = dot(fit, fit, (1, 1), EXACT)
        trace = jnp.sum(jnp.where(diagonal, gram, 0.0), keepdims=True)
        ridge = ridge_share * trace / keep
        bound = trace + ridge
        fits.append(fit)
        system = (gram + ridge * unit) / bound
        pairs.append((system, unit / bound))
    lows = spectrum_steps(keep)
    for step, low in enumerate(lows):
        gain = 4.0 / (1.0 + low) ** 2
        for j in range(ipl):
            system, inverse = pairs[j]
            factor = gain * (1.0 + low) * unit - gain * system
            if step == len(lows) - 1:
                fit_map[j] = product(factor, product(inverse, fits[j]))
            else:
                both = product(factor, jnp.concatenate([system, inverse], axis=1))
                pairs[j] = (both[:, :keep], both[:, keep:])

    pass_on(key_copy, key_order)
    merge(0)
    for j in range(ipl):
        target = own_sum[0, j] / own_stats[0, 1, pl.ds(j, 1), :]
        out_values[me * ipl + j] = dot(fit_map[j], target, (1, 1), EXACT).astype(bf16)

    own_on(value_copy, value_order)
    pass_on(value_copy, value_order)
    finish(key_copy, key_order)
    finish(value_copy, value_order)


def shards(cache_keys, cache_values, ref_queries, listed):
    layer_count, head_count, tok, head = cache_keys.shape
    query_count, keep = ref_queries.shape[2], listed.shape[2]
    items = layer_count * head_count
    n = lax.axis_size("ctx")
    ipl = items // n
    vmem = pl.BlockSpec(memory_space=pltpu.VMEM)
    dma = pltpu.SemaphoreType.DMA
    out = jax.ShapeDtypeStruct((items, keep, head), bf16)
    sums = (ipl, head, query_count)
    stats = (2, ipl, query_count)
    held = [
        pltpu.VMEM((items, tok, head), bf16),
        pltpu.VMEM((items, tok, head), bf16),
        pltpu.VMEM((items, query_count, head), bf16),
    ]
    scratch = held + [
        pltpu.VMEM((items, keep), jnp.int32),
        pltpu.VMEM((items, keep), f32),
        pltpu.VMEM((n, ipl, block_rows, head), bf16),
        pltpu.VMEM((n, ipl, block_rows, head), bf16),
        pltpu.VMEM((n // 2,) + sums, f32),
        pltpu.VMEM((n // 2,) + stats, f32),
        pltpu.VMEM((n,) + sums, bf16),
        pltpu.VMEM((n,) + sums, bf16),
        pltpu.VMEM((n,) + stats, f32),
        pltpu.VMEM((n,) + stats, f32),
        pltpu.VMEM((ipl, keep, query_count), f32),
    ]
    scratch += [dma((n,))] * 10 + [dma((3, n))]
    compact, solved = pl.pallas_call(
        functools.partial(kernel, n),
        out_shape=(out, out),
        in_specs=[pl.BlockSpec(memory_space=pl.ANY)] * 3 + [vmem],
        out_specs=(vmem, vmem),
        scratch_shapes=scratch,
        compiler_params=pltpu.CompilerParams(
            collective_id=0, has_side_effects=True, vmem_limit_bytes=48 * 2**20
        ),
        name="compact_fit",
    )(
        cache_keys.reshape(items, tok, head),
        cache_values.reshape(items, tok, head),
        ref_queries.reshape(items, query_count, head),
        listed.reshape(items, keep),
    )
    shape = (layer_count, head_count, keep, head)
    return compact.reshape(shape), solved.reshape(shape)


def solution(mesh):
    in_specs = (
        P("grp", "head", "ctx", None),
        P("grp", "head", "ctx", None),
        P("grp", "head", None, None),
        P("grp", "head", None),
    )
    out_specs = (P("grp", "head", None, None), P("grp", "head", None, None))
    return jax.shard_map(shards, mesh=mesh, in_specs=in_specs, out_specs=out_specs, check_vma=False)
```
